32 devices in a mesh: segment: 4 (over z), dp: 4 (over y, x), expert: 2 (over core).
Axes of the slice: x: 2, y: 2, z: 4, core: 2. Of those that a mesh axis runs over, the one named last changes fastest.
Arguments:
- fwd_inputs: bfloat16 [4, 512, 2048], P('segment', ('dp', 'expert')), may hold values from -17 to 17
- fwd_routes: int32 [4, 512, 8], P('segment', ('dp', 'expert')), may hold values from 0 to 15, as said below
- fwd_weights: float32 [4, 512, 8], P('segment', ('dp', 'expert')), may hold values from 0.2 to 0.6
- bwd_inputs: bfloat16 [4, 512, 2048], P('segment', ('dp', 'expert')), may hold values from -17 to 17
- bwd_cotangent: bfloat16 [4, 512, 2048], P('segment', ('dp', 'expert')), may hold values from -6 to 6
- bwd_routes: int32 [4, 512, 8], P('segment', ('dp', 'expert')), may hold values from 0 to 15, as said below
- bwd_weights: float32 [4, 512, 8], P('segment', ('dp', 'expert')), may hold values from 0.2 to 0.6
- norm_gain: float32 [4, 2048], P('segment'), may hold values from 0.5 to 2
- w_gate: bfloat16 [4, 16, 2048, 384], P('segment', ('dp', 'expert')), may hold values from -0.125 to 0.125
- w_up: bfloat16 [4, 16, 2048, 384], P('segment', ('dp', 'expert')), may hold values from -0.125 to 0.125
- w_down: bfloat16 [4, 16, 384, 2048], P('segment', ('dp', 'expert')), may hold values from -0.3125 to 0.3125
Outputs:
- next_forward: bfloat16 [4, 512, 2048], P('segment', ('dp', 'expert'))
- prev_grad: bfloat16 [4, 512, 2048], P('segment', ('dp', 'expert'))
The draws below stay inside these ranges and needn't reach their ends.
Inputs may be any that keep to these rules, and one draw needn't show every extreme that they name: `fwd_routes`: each row names 8 different experts. Among the rows of one device no expert is named more than 36 times, and in each section one expert is named exactly 36 times on every device of that section. `bwd_routes`: each row names 8 different experts. Among the rows of one device no expert is named more than 36 times, and in each section one expert is named exactly 36 times on every device of that section.
All inputs are finite; a program needn't handle non-finite values.
Results may differ from the reference program's by a relative error of at most 0.0059.
Values may be sent and summed in bfloat16 or wider, within the bound.
A program may use at most 128 MiB of HBM per device.

```python
import math
import jax
import jax.numpy as jnp
from jax import lax

D = 2048
TOPK = 8
FFE = 384
TOK_DEV = 64
SEGMENTS = 4
EXPERTS = 16
TOKENS = 512
CAP = 36
N_DP = 4
N_EXPERT = 2


def route_table(base_key):
    blocks_count = TOKENS // TOK_DEV
    entries = TOK_DEV * TOPK
    tickets = EXPERTS * CAP

    def one_segment(segment_key):
        first_key, second_key, third_key, fourth_key = jax.random.split(segment_key, 4)
        expert_bias = jax.random.randint(first_key, (EXPERTS,), 0, 48)
        hot_expert = jax.random.randint(second_key, (), 0, EXPERTS)
        rename = jax.random.permutation(third_key, EXPERTS).astype(jnp.int32)
        owners = jnp.arange(tickets, dtype=jnp.int32) // CAP

        def one_block(block_key):
            noise_key, order_key = jax.random.split(block_key)
            priority = jax.random.randint(noise_key, (tickets,), 0, 32) + expert_bias[owners] + 1000 * (owners == hot_expert).astype(jnp.int32)
            ranked = priority * tickets + jnp.arange(tickets, dtype=jnp.int32)
            unused, chosen = lax.top_k(ranked, entries)
            chosen = jnp.sort(chosen)
            experts_list = rename[chosen // CAP]
            layout = experts_list.reshape(TOPK, TOK_DEV).T
            row_order = jax.random.permutation(order_key, TOK_DEV)
            return layout[row_order]
        tables = jax.vmap(one_block)(jax.random.split(fourth_key, blocks_count))
        return tables.reshape(TOKENS, TOPK)
    return jax.vmap(one_segment)(jax.random.split(base_key, SEGMENTS)).astype(jnp.int32)


def activation_field(base_key):
    first_key, second_key, third_key = jax.random.split(base_key, 3)
    shape_full = (SEGMENTS, TOKENS, D)
    basis = jnp.clip(jax.random.normal(first_key, shape_full, jnp.float32), -4.0, 4.0)
    row_scale = jnp.exp(jax.random.uniform(second_key, (SEGMENTS, TOKENS, 1), jnp.float32, -0.7, 0.7))
    column_scale = jnp.exp(jax.random.uniform(third_key, (D,), jnp.float32, -0.7, 0.7))
    return (basis * row_scale * column_scale).astype(jnp.bfloat16)


def draw_fwd_routes(key, part):
    return route_table(jax.random.fold_in(key, 11))


def draw_bwd_routes(key, part):
    return route_table(jax.random.fold_in(key, 23))


def draw_fwd_inputs(key, part):
    return activation_field(jax.random.fold_in(key, 37))


def draw_bwd_inputs(key, part):
    return activation_field(jax.random.fold_in(key, 41))


def block_levels(stream_key, extent, cuts, least, top_value):
    loudness, own = 1.0, jax.random.fold_in(stream_key, 6)
    for axis_at, shards_of in cuts:
        draws = jnp.exp(jax.random.uniform(jax.random.fold_in(own, axis_at), (shards_of,), jnp.float32, least / len(cuts), top_value / len(cuts)))
        loudness = loudness * jnp.repeat(draws, extent[axis_at] // shards_of).reshape([-1 if axis == axis_at else 1 for axis in range(len(extent))])
    return loudness


def noise(own_key, shape, width, most, cuts=(), kind=jnp.bfloat16):
    gain = block_levels(own_key, shape, cuts, -0.22, 0.18) if cuts else 1.0
    result = jax.random.normal(own_key, shape, jnp.float32) * width * gain
    return jnp.minimum(jnp.maximum(result, -most), most).astype(kind)


def setup_inputs(seed: int = 0) -> dict:
    streams_of = jax.random.split(jax.random.key(seed), 12)
    return {
        "fwd_inputs": draw_fwd_inputs(jax.random.fold_in(streams_of[11], 71), 0),
        "fwd_routes": draw_fwd_routes(jax.random.fold_in(streams_of[11], 71), 0),
        "fwd_weights": jnp.clip(0.2 + 0.400000021 * jax.random.uniform(streams_of[2], (SEGMENTS, TOKENS, TOPK), jnp.float32) ** block_levels(streams_of[2], (SEGMENTS, TOKENS, TOPK), ((0, 4), (1, 8)), -0.2, 0.2), 0.2, 0.6),
        "bwd_inputs": draw_bwd_inputs(jax.random.fold_in(streams_of[11], 71), 0),
        "bwd_cotangent": noise(streams_of[4], (SEGMENTS, TOKENS, D), 1.0, 6.0, ((0, 4), (1, 8))),
        "bwd_routes": draw_bwd_routes(jax.random.fold_in(streams_of[11], 71), 0),
        "bwd_weights": jnp.clip(0.2 + 0.400000021 * jax.random.uniform(streams_of[6], (SEGMENTS, TOKENS, TOPK), jnp.float32) ** block_levels(streams_of[6], (SEGMENTS, TOKENS, TOPK), ((0, 4), (1, 8)), -0.2, 0.2), 0.2, 0.6),
        "norm_gain": jnp.clip(jnp.exp(math.log(2.0) - 1.3862944 * jax.random.uniform(streams_of[7], (SEGMENTS, D), jnp.float32) ** block_levels(streams_of[7], (SEGMENTS, D), ((0, 4),), -0.2, 0.2)), 0.5, 2.0),
        "w_gate": noise(streams_of[8], (SEGMENTS, EXPERTS, D, FFE), D ** -0.5, 0.125, ((0, 4), (1, 8))),
        "w_up": noise(streams_of[9], (SEGMENTS, EXPERTS, D, FFE), D ** -0.5, 0.125, ((0, 4), (1, 8))),
        "w_down": noise(streams_of[10], (SEGMENTS, EXPERTS, FFE, D), FFE ** -0.5, 0.3125, ((0, 4), (1, 8))),
    }


EPSILON = 1e-06

def normalize(inputs, norm_scale):
    values = inputs.astype(jnp.float32)
    inv_rms = lax.rsqrt(lax.optimization_barrier(jnp.mean(values * values, axis=-1, keepdims=True)) + EPSILON)
    return ((values * inv_rms * norm_scale).astype(jnp.bfloat16), values, inv_rms)

def expert_rows(normed_rows, back_rows, cotangent_rows, gate_mat, up_mat, down_mat):
    gate_proj = jnp.dot(normed_rows, gate_mat, preferred_element_type=jnp.float32)
    up_proj = jnp.dot(normed_rows, up_mat, preferred_element_type=jnp.float32)
    activated = (gate_proj * jax.nn.sigmoid(gate_proj) * up_proj).astype(jnp.bfloat16)
    out_rows = jnp.dot(activated, down_mat, preferred_element_type=jnp.float32).astype(jnp.bfloat16)
    gate_back = jnp.dot(back_rows, gate_mat, preferred_element_type=jnp.float32)
    up_back = jnp.dot(back_rows, up_mat, preferred_element_type=jnp.float32)
    back_hidden = jnp.dot(cotangent_rows, down_mat.T, preferred_element_type=jnp.float32)
    sigmoid_gate = jax.nn.sigmoid(gate_back)
    d_gate = (back_hidden * up_back * sigmoid_gate * (1.0 + gate_back * (1.0 - sigmoid_gate))).astype(jnp.bfloat16)
    d_up = (back_hidden * gate_back * sigmoid_gate).astype(jnp.bfloat16)
    d_normed = (jnp.dot(d_gate, gate_mat.T, preferred_element_type=jnp.float32) + jnp.dot(d_up, up_mat.T, preferred_element_type=jnp.float32)).astype(jnp.bfloat16)
    return (out_rows, d_normed)

def section(fwd_inputs, fwd_routes, fwd_weights, bwd_inputs, bwd_cotangent, bwd_routes, bwd_weights, norm_scale, w_gate, w_up, w_down):
    normed_fwd = normalize(fwd_inputs, norm_scale)[0]
    normed_bwd, back_values, back_rms = normalize(bwd_inputs, norm_scale)
    entries = TOKENS * TOPK
    most_rows = N_DP * N_EXPERT * CAP
    fwd_flat = fwd_routes.reshape(-1)
    bwd_flat = bwd_routes.reshape(-1)
    fwd_factors = fwd_weights.reshape(-1)
    bwd_factors = bwd_weights.reshape(-1)

    def visit(carry, member):
        expert_id, gate_mat, up_mat, down_mat = member
        acc_fwd, acc_bwd = carry
        fwd_index = jnp.nonzero(fwd_flat == expert_id, size=most_rows, fill_value=entries)[0].astype(jnp.int32)
        bwd_index = jnp.nonzero(bwd_flat == expert_id, size=most_rows, fill_value=entries)[0].astype(jnp.int32)
        fwd_clip = jnp.minimum(fwd_index, entries - 1)
        bwd_clip = jnp.minimum(bwd_index, entries - 1)
        fwd_token = fwd_clip // TOPK
        bwd_token = bwd_clip // TOPK
        out_rows, d_rows = expert_rows(normed_fwd[fwd_token], normed_bwd[bwd_token], bwd_cotangent[bwd_token], gate_mat, up_mat, down_mat)
        fwd_scale = jnp.where(fwd_index < entries, fwd_factors[fwd_clip], jnp.zeros_like(fwd_factors[fwd_clip]))
        bwd_scale = jnp.where(bwd_index < entries, bwd_factors[bwd_clip], jnp.zeros_like(bwd_factors[bwd_clip]))
        acc_fwd = acc_fwd.at[fwd_token].add(out_rows.astype(jnp.float32) * fwd_scale[:, None])
        acc_bwd = acc_bwd.at[bwd_token].add(d_rows.astype(jnp.float32) * bwd_scale[:, None])
        return ((acc_fwd, acc_bwd), None)
    start = (jnp.zeros((TOKENS, D), jnp.float32), jnp.zeros((TOKENS, D), jnp.float32))
    members = (jnp.arange(EXPERTS, dtype=jnp.int32), w_gate, w_up, w_down)
    (combined, norm_grad), unused = lax.scan(visit, start, members)
    section_out = (fwd_inputs.astype(jnp.float32) + combined).astype(jnp.bfloat16)
    scaled = norm_scale * norm_grad
    section_grad = (bwd_cotangent.astype(jnp.float32) + back_rms * scaled - back_values * back_rms ** 3 * lax.optimization_barrier(jnp.mean(back_values * scaled, axis=-1, keepdims=True))).astype(jnp.bfloat16)
    return (section_out, section_grad)

def reference(fwd_inputs, fwd_routes, fwd_weights, bwd_inputs, bwd_cotangent, bwd_routes, bwd_weights, norm_gain, w_gate, w_up, w_down):
    outs_list = []
    grads_list = []
    for segment_id in range(SEGMENTS):
        section_out, section_grad = section(fwd_inputs[segment_id], fwd_routes[segment_id], fwd_weights[segment_id], bwd_inputs[segment_id], bwd_cotangent[segment_id], bwd_routes[segment_id], bwd_weights[segment_id], norm_gain[segment_id], w_gate[segment_id], w_up[segment_id], w_down[segment_id])
        outs_list.append(section_out)
        grads_list.append(section_grad)
    next_forward = jnp.roll(jnp.stack(outs_list), 1, axis=0)
    prev_grad = jnp.roll(jnp.stack(grads_list), -1, axis=0)
    return (next_forward, prev_grad)
```

```python
import jax
import jax.numpy as jnp
from jax import lax
from jax.sharding import PartitionSpec as P

EPSILON = 1e-06
GROUP = ("dp", "expert")
BLOCKS = 8


def from_behind(value, axis, steps):
    count = lax.axis_size(axis)
    pairs = [(source, (source + steps) % count) for source in range(count)]
    return lax.ppermute(value, axis, pairs)


def normalize(inputs, norm_scale):
    values = inputs.astype(jnp.float32)
    inv_rms = lax.rsqrt(jnp.mean(values * values, axis=-1, keepdims=True) + EPSILON)
    return ((values * inv_rms * norm_scale).astype(jnp.bfloat16), values, inv_rms)


def dense_weights(routes, weights, experts_total):
    onehot = routes[:, :, None] == jnp.arange(experts_total, dtype=jnp.int32)
    return jnp.sum(jnp.where(onehot, weights[:, :, None], 0.0), axis=1)


def dot(a, b):
    return jnp.dot(a, b, preferred_element_type=jnp.float32)


def dot_t(a, b):
    return lax.dot_general(a, b, (((1,), (1,)), ((), ())), preferred_element_type=jnp.float32)


def by_blocks(work, block, *operands):
    count = operands[0].shape[0] // block
    if count == 1:
        return work(*operands)
    cut = [value.reshape(count, block, *value.shape[1:]) for value in operands]
    made = lax.map(lambda parts: work(*parts), tuple(cut))
    return made.reshape(count * block, made.shape[-1])


def body(
    fwd_inputs,
    fwd_routes,
    fwd_weights,
    bwd_inputs,
    bwd_cotangent,
    bwd_routes,
    bwd_weights,
    norm_gain,
    w_gate,
    w_up,
    w_down,
):
    local_experts = w_gate.shape[1]
    experts_total = local_experts * lax.axis_size("dp") * lax.axis_size("expert")
    first = local_experts * (lax.axis_index("dp") * lax.axis_size("expert") + lax.axis_index("expert"))
    norm_scale = norm_gain[0]
    both = jnp.stack(
        [
            dense_weights(fwd_routes[0], fwd_weights[0], experts_total),
            dense_weights(bwd_routes[0], bwd_weights[0], experts_total),
        ],
        axis=1,
    )
    both = lax.all_gather(both, GROUP, axis=0, tiled=True)
    both = lax.dynamic_slice_in_dim(both, first, local_experts, axis=2)
    normed_fwd = normalize(fwd_inputs[0], norm_scale)[0]
    normed_bwd, back_values, back_rms = normalize(bwd_inputs[0], norm_scale)
    fwd_rows = lax.all_gather(normed_fwd, GROUP, axis=0, tiled=True)
    bwd_rows = lax.all_gather(normed_bwd, GROUP, axis=0, tiled=True)
    cot_rows = lax.all_gather(bwd_cotangent[0], GROUP, axis=0, tiled=True)

    def forward(rows, factors):
        partial = 0.0
        for e in range(local_experts):
            gate = dot(rows, w_gate[0, e])
            up = dot(rows, w_up[0, e])
            act = gate * jax.nn.sigmoid(gate) * up * factors[:, e : e + 1]
            partial = partial + dot(act.astype(jnp.bfloat16), w_down[0, e])
        return partial.astype(jnp.bfloat16)

    def backward(rows, cotangents, factors):
        partial = 0.0
        for e in range(local_experts):
            gate = dot(rows, w_gate[0, e])
            up = dot(rows, w_up[0, e])
            hidden = dot_t(cotangents, w_down[0, e]) * factors[:, e : e + 1]
            q = jax.nn.sigmoid(gate)
            d_gate = (hidden * up * q * (1.0 + gate * (1.0 - q))).astype(jnp.bfloat16)
            d_up = (hidden * gate * q).astype(jnp.bfloat16)
            partial = partial + dot_t(d_gate, w_gate[0, e]) + dot_t(d_up, w_up[0, e])
        return partial.astype(jnp.bfloat16)

    block = BLOCKS * fwd_inputs.shape[1]
    partial = by_blocks(forward, block, fwd_rows, both[:, 0])
    combined = lax.psum_scatter(partial, GROUP, scatter_dimension=0, tiled=True)
    section_out = (fwd_inputs[0].astype(jnp.float32) + combined.astype(jnp.float32)).astype(jnp.bfloat16)
    next_forward = from_behind(section_out[None], "segment", 1)

    partial = by_blocks(backward, block, bwd_rows, cot_rows, both[:, 1])
    norm_grad = lax.psum_scatter(
        partial, GROUP, scatter_dimension=0, tiled=True
    ).astype(jnp.float32)
    scaled = norm_scale * norm_grad
    section_grad = (
        bwd_cotangent[0].astype(jnp.float32)
        + back_rms * scaled
        - back_values * back_rms**3 * jnp.mean(back_values * scaled, axis=-1, keepdims=True)
    ).astype(jnp.bfloat16)
    prev_grad = from_behind(section_grad[None], "segment", -1)
    return (next_forward, prev_grad)


def solution(mesh):
    rows = P("segment", GROUP, None)
    wide = P("segment", GROUP, None, None)
    return jax.shard_map(
        body,
        mesh=mesh,
        in_specs=(rows,) * 7 + (P("segment", None),) + (wide,) * 3,
        out_specs=(rows, rows),
        check_vma=False,
    )
```

```python
import functools

import jax
import jax.numpy as jnp
from jax import lax
from jax.experimental import pallas as pl
from jax.experimental.pallas import tpu as pltpu
from jax.sharding import PartitionSpec as P

EPSILON = 1e-06
GROUP = ("dp", "expert")
BLOCKS = 8


def from_behind(value, axis, steps):
    count = lax.axis_size(axis)
    pairs = [(source, (source + steps) % count) for source in range(count)]
    return lax.ppermute(value, axis, pairs)


def normalize(inputs, norm_scale):
    values = inputs.astype(jnp.float32)
    inv_rms = lax.rsqrt(jnp.mean(values * values, axis=-1, keepdims=True) + EPSILON)
    return ((values * inv_rms * norm_scale).astype(jnp.bfloat16), values, inv_rms)


def dense_weights(routes, weights, experts_total):
    onehot = routes[:, :, None] == jnp.arange(experts_total, dtype=jnp.int32)
    return jnp.sum(jnp.where(onehot, weights[:, :, None], 0.0), axis=1)


def dot(a, b):
    return jnp.dot(a, b, preferred_element_type=jnp.float32)


def dot_t(a, b):
    return lax.dot_general(a, b, (((1,), (1,)), ((), ())), preferred_element_type=jnp.float32)


def by_blocks(work, block, *operands):
    count = operands[0].shape[0] // block
    if count == 1:
        return work(*operands)
    cut = [value.reshape(count, block, *value.shape[1:]) for value in operands]
    made = lax.map(lambda parts: work(*parts), tuple(cut))
    return made.reshape(count * block, made.shape[-1])


def body(
    fwd_inputs,
    fwd_routes,
    fwd_weights,
    bwd_inputs,
    bwd_cotangent,
    bwd_routes,
    bwd_weights,
    norm_gain,
    w_gate,
    w_up,
    w_down,
):
    local_experts = w_gate.shape[1]
    experts_total = local_experts * lax.axis_size("dp") * lax.axis_size("expert")
    first = local_experts * (lax.axis_index("dp") * lax.axis_size("expert") + lax.axis_index("expert"))
    norm_scale = norm_gain[0]
    both = jnp.stack(
        [
            dense_weights(fwd_routes[0], fwd_weights[0], experts_total),
            dense_weights(bwd_routes[0], bwd_weights[0], experts_total),
        ],
        axis=1,
    )
    both = lax.all_gather(both, GROUP, axis=0, tiled=True)
    both = lax.dynamic_slice_in_dim(both, first, local_experts, axis=2)
    normed_fwd = normalize(fwd_inputs[0], norm_scale)[0]
    normed_bwd, back_values, back_rms = normalize(bwd_inputs[0], norm_scale)
    fwd_rows = lax.all_gather(normed_fwd, GROUP, axis=0, tiled=True)
    bwd_rows = lax.all_gather(normed_bwd, GROUP, axis=0, tiled=True)
    cot_rows = lax.all_gather(bwd_cotangent[0], GROUP, axis=0, tiled=True)

    def forward(rows, factors):
        partial = 0.0
        for e in range(local_experts):
            gate = dot(rows, w_gate[0, e])
            up = dot(rows, w_up[0, e])
            act = gate * jax.nn.sigmoid(gate) * up * factors[:, e : e + 1]
            partial = partial + dot(act.astype(jnp.bfloat16), w_down[0, e])
        return partial.astype(jnp.bfloat16)

    def backward(rows, cotangents, factors):
        partial = 0.0
        for e in range(local_experts):
            gate = dot(rows, w_gate[0, e])
            up = dot(rows, w_up[0, e])
            hidden = dot_t(cotangents, w_down[0, e]) * factors[:, e : e + 1]
            q = jax.nn.sigmoid(gate)
            d_gate = (hidden * up * q * (1.0 + gate * (1.0 - q))).astype(jnp.bfloat16)
            d_up = (hidden * gate * q).astype(jnp.bfloat16)
            partial = partial + dot_t(d_gate, w_gate[0, e]) + dot_t(d_up, w_up[0, e])
        return partial.astype(jnp.bfloat16)

    block = BLOCKS * fwd_inputs.shape[1]
    partial = by_blocks(forward, block, fwd_rows, both[:, 0])
    combined = lax.psum_scatter(partial, GROUP, scatter_dimension=0, tiled=True)
    section_out = (fwd_inputs[0].astype(jnp.float32) + combined.astype(jnp.float32)).astype(jnp.bfloat16)
    next_forward = from_behind(section_out[None], "segment", 1)

    partial = by_blocks(backward, block, bwd_rows, cot_rows, both[:, 1])
    norm_grad = lax.psum_scatter(
        partial, GROUP, scatter_dimension=0, tiled=True
    ).astype(jnp.float32)
    scaled = norm_scale * norm_grad
    section_grad = (
        bwd_cotangent[0].astype(jnp.float32)
        + back_rms * scaled
        - back_values * back_rms**3 * jnp.mean(back_values * scaled, axis=-1, keepdims=True)
    ).astype(jnp.bfloat16)
    prev_grad = from_behind(section_grad[None], "segment", -1)
    return (next_forward, prev_grad)


LANES = 128
VMEM_BYTES = 52 * 2**20


def remote(src, dst, send, recv, device):
    return pltpu.make_async_remote_copy(
        src_ref=src, dst_ref=dst, send_sem=send, recv_sem=recv,
        device_id=device, device_id_type=pl.DeviceIdType.MESH,
    )


def kernel(
    n_seg, n_dp, experts_total,
    fwd_ref, froute_ref, fweight_ref, bwd_ref, cot_ref, broute_ref, bweight_ref, gain_ref,
    gate_hbm, up_hbm, down_hbm, next_ref, prev_ref,
    gate_w, up_w, down_w, rows, factors, part, mate, summed, landed, hidden, act_a, act_b, outs,
    load_sem, fac_send, fac_recv, row_send, row_recv, mate_send, mate_recv,
    psend, precv, qsend, qrecv, shift_send, shift_recv,
):
    seg, dp, ex = lax.axis_index("segment"), lax.axis_index("dp"), lax.axis_index("expert")
    me = dp * 2 + ex
    group = n_dp * 2
    other = 1 - ex
    tokens, width = cot_ref.shape
    local, _, inner = gate_w.shape
    ahead, behind = lax.rem(seg + 1, n_seg), lax.rem(seg + n_seg - 1, n_seg)

    loads = [
        pltpu.make_async_copy(src, dst, load_sem.at[i])
        for i, (src, dst) in enumerate(((down_hbm, down_w), (gate_hbm, gate_w), (up_hbm, up_w)))
    ]
    for copy in loads:
        copy.start()

    def member(k):
        p = lax.rem(me + k, group)
        return (seg, p // 2, lax.rem(p, 2))

    barrier = pltpu.get_barrier_semaphore()
    for k in range(1, group):
        pl.semaphore_signal(barrier, inc=1, device_id=member(k), device_id_type=pl.DeviceIdType.MESH)
    for s in (ahead, behind):
        pl.semaphore_signal(barrier, inc=1, device_id=(s, dp, ex), device_id_type=pl.DeviceIdType.MESH)
    pl.semaphore_wait(barrier, group + 1)

    def start_rows(t):
        copies = []
        own = rows.at[t, dp, ex]
        for k in range(1, n_dp):
            copies.append(remote(own, own, row_send.at[t, k], row_recv.at[t, k], (seg, lax.rem(dp + k, n_dp), ex)))
        copies.append(remote(own, own, mate_send.at[t, 0], mate_recv.at[t, 0], (seg, dp, other)))
        for copy in copies:
            copy.start()
        return copies

    def finish_rows(t, copies):
        passed = [copies[-1]]
        for k in range(1, n_dp):
            copies[k - 1].wait_recv()
            slot = rows.at[t, lax.rem(dp + n_dp - k, n_dp), ex]
            copy = remote(slot, slot, mate_send.at[t, k], mate_recv.at[t, k], (seg, dp, other))
            copy.start()
            passed.append(copy)
        for copy in passed:
            copy.wait_recv()
        return copies[:-1] + passed

    rows[0, dp, ex] = cot_ref[...]
    cot_copies = start_rows(0)
    rows[1, dp, ex] = normalize(bwd_ref[...], gain_ref[...])[0]
    bwd_copies = start_rows(1)

    lane = lax.broadcasted_iota(jnp.int32, (tokens, LANES), 1)
    dense = jnp.zeros((tokens, LANES), jnp.float32)
    for base, routes, weights in ((0, froute_ref, fweight_ref), (experts_total, broute_ref, bweight_ref)):
        for k in range(routes.shape[1]):
            hit = lane == routes[:, k : k + 1] + base
            dense = dense + jnp.where(hit, weights[:, k : k + 1], 0.0)
    factors[me] = dense
    fac_copies = [
        remote(factors.at[me], factors.at[me], fac_send.at[k], fac_recv.at[k], member(k)) for k in range(1, group)
    ]
    for copy in fac_copies:
        copy.start()
    rows[2, dp, ex] = normalize(fwd_ref[...], gain_ref[...])[0]
    fwd_copies = start_rows(2)

    pair = 2 * tokens

    def column(d, base, e):
        table = factors[pl.ds(d * 2, 2)].reshape(pair, LANES)
        spot = lax.broadcasted_iota(jnp.int32, (pair, LANES), 1) == base + me * local + e
        return jnp.sum(jnp.where(spot, table, 0.0), axis=1, keepdims=True)

    def scatter(t, product):
        mates, sent = [None] * n_dp, []

        def pass_on(k):
            q = lax.rem(dp + k, n_dp)
            mates[k].wait_recv()
            if k:
                both = part[t, q, ex].astype(jnp.float32) + mate[t, q].astype(jnp.float32)
                summed[t, k] = both.astype(jnp.bfloat16)
                copy = remote(summed.at[t, k], landed.at[t, k], qsend.at[t, k], qrecv.at[t, k], (seg, q, ex))
                copy.start()
                sent.append(copy)

        order = list(range(1, n_dp)) + [0]
        for i, k in enumerate(order):
            q = lax.rem(dp + k, n_dp)
            product(q)
            mates[k] = remote(
                part.at[t, q, other], mate.at[t, q], psend.at[t, k], precv.at[t, k], (seg, dp, other)
            )
            mates[k].start()
            if i:
                pass_on(order[i - 1])
        pass_on(order[-1])
        return mates, sent

    tile = 512 if width % 512 == 0 else LANES

    def tiles(t, q, make):
        def step(i, carry):
            at = pl.ds(pl.multiple_of(i * tile, tile), tile)
            made = make(q, at).astype(jnp.bfloat16)
            part[t, q, :, :, at] = made.reshape(2, tokens, tile)
            return carry

        lax.fori_loop(0, width // tile, step, 0)

    def each(work):
        def step(i, carry):
            work(i // local, lax.rem(i, local))
            return carry

        lax.fori_loop(0, n_dp * local, step, 0)

    def cot_work(d, e):
        hidden[d, e] = dot_t(rows[0, d].reshape(pair, width), down_w[e])

    def bwd_work(d, e):
        x = rows[1, d].reshape(pair, width)
        gate, up = dot(x, gate_w[e]), dot(x, up_w[e])
        back = hidden[d, e] * column(d, experts_total, e)
        q = jax.nn.sigmoid(gate)
        act_a[d, e] = (back * up * q * (1.0 + gate * (1.0 - q))).astype(jnp.bfloat16)
        act_b[d, e] = (back * gate * q).astype(jnp.bfloat16)

    def bwd_product(q):
        def make(q, at):
            total = 0.0
            for e in range(local):
                total = total + dot_t(act_a[q, e], gate_w[e, at, :]) + dot_t(act_b[q, e], up_w[e, at, :])
            return total

        tiles(0, q, make)

    def fwd_work(d, e):
        x = rows[2, d].reshape(pair, width)
        gate, up = dot(x, gate_w[e]), dot(x, up_w[e])
        act_a[d, e] = (gate * jax.nn.sigmoid(gate) * up * column(d, 0, e)).astype(jnp.bfloat16)

    def fwd_product(q):
        def make(q, at):
            total = 0.0
            for e in range(local):
                total = total + dot(act_a[q, e], down_w[e, :, at])
            return total

        tiles(1, q, make)

    def gathered(t, sent):
        total = part[t, dp, ex].astype(jnp.float32) + mate[t, dp].astype(jnp.float32)
        for copy in sent:
            copy.wait_recv()
        for k in range(1, n_dp):
            total = total + landed[t, k].astype(jnp.float32)
        return total

    cot_copies = finish_rows(0, cot_copies)
    loads[0].wait()
    each(cot_work)
    bwd_copies = finish_rows(1, bwd_copies)
    for copy in fac_copies:
        copy.wait_recv()
    loads[1].wait()
    loads[2].wait()
    each(bwd_work)
    bwd_mates, bwd_sent = scatter(0, bwd_product)

    fwd_copies = finish_rows(2, fwd_copies)
    each(fwd_work)
    fwd_mates, fwd_sent = scatter(1, fwd_product)

    scaled = gain_ref[...] * gathered(0, bwd_sent)
    _, values, inv_rms = normalize(bwd_ref[...], gain_ref[...])
    mean = jnp.mean(values * scaled, axis=-1, keepdims=True)
    outs[0] = (cot_ref[...].astype(jnp.float32) + inv_rms * scaled - values * inv_rms**3 * mean).astype(jnp.bfloat16)
    back = remote(outs.at[0], prev_ref, shift_send.at[0], shift_recv.at[0], (behind, dp, ex))
    back.start()
    outs[1] = (fwd_ref[...].astype(jnp.float32) + gathered(1, fwd_sent)).astype(jnp.bfloat16)
    on = remote(outs.at[1], next_ref, shift_send.at[1], shift_recv.at[1], (ahead, dp, ex))
    on.start()
    for copy in cot_copies + bwd_copies + fwd_copies + fac_copies + bwd_mates + fwd_mates + bwd_sent + fwd_sent:
        copy.wait_send()
    back.wait()
    on.wait()


def fused(n_seg, n_dp, *operands):
    flat = [value[0] for value in operands]
    flat[7] = operands[7]
    tokens, width = flat[0].shape
    local, _, inner = flat[8].shape
    wide, dma = jnp.bfloat16, pltpu.SemaphoreType.DMA
    block = (tokens, width)
    out = jax.ShapeDtypeStruct(block, wide)
    vmem = pl.BlockSpec(memory_space=pltpu.VMEM)
    group = 2 * n_dp
    made = pl.pallas_call(
        functools.partial(kernel, n_seg, n_dp, group * local),
        out_shape=(out, out),
        in_specs=[vmem] * 8 + [pl.BlockSpec(memory_space=pl.ANY)] * 3,
        out_specs=(vmem, vmem),
        scratch_shapes=[
            pltpu.VMEM(flat[8].shape, wide),
            pltpu.VMEM(flat[9].shape, wide),
            pltpu.VMEM(flat[10].shape, wide),
            pltpu.VMEM((3, n_dp, 2) + block, wide),
            pltpu.VMEM((group, tokens, LANES), jnp.float32),
            pltpu.VMEM((2, n_dp, 2) + block, wide),
            pltpu.VMEM((2, n_dp) + block, wide),
            pltpu.VMEM((2, n_dp) + block, wide),
            pltpu.VMEM((2, n_dp) + block, wide),
            pltpu.VMEM((n_dp, local, 2 * tokens, inner), jnp.float32),
            pltpu.VMEM((n_dp, local, 2 * tokens, inner), wide),
            pltpu.VMEM((n_dp, local, 2 * tokens, inner), wide),
            pltpu.VMEM((2,) + block, wide),
            dma((3,)), dma((group,)), dma((group,)),
            dma((3, n_dp)), dma((3, n_dp)), dma((3, n_dp)), dma((3, n_dp)),
            dma((2, n_dp)), dma((2, n_dp)), dma((2, n_dp)), dma((2, n_dp)),
            dma((2,)), dma((2,)),
        ],
        compiler_params=pltpu.CompilerParams(
            collective_id=0, has_side_effects=True, vmem_limit_bytes=VMEM_BYTES
        ),
    )(*flat)
    return (made[0][None], made[1][None])


def whole(n_seg, n_dp, n_expert, *operands):
    tokens, width = operands[0].shape[1:]
    local = operands[8].shape[1]
    group = n_dp * n_expert
    rows_bytes = group * tokens * width * 2
    small = 9 * rows_bytes + 3 * operands[8].size * 2 <= VMEM_BYTES * 3 // 4
    if n_expert == 2 and n_dp > 1 and n_seg > 1 and 2 * group * local <= LANES and small:
        return fused(n_seg, n_dp, *operands)
    return body(*operands)


def solution(mesh):
    rows = P("segment", GROUP, None)
    wide = P("segment", GROUP, None, None)
    return jax.shard_map(
        functools.partial(whole, mesh.shape["segment"], mesh.shape["dp"], mesh.shape["expert"]),
        mesh=mesh,
        in_specs=(rows,) * 7 + (P("segment", None),) + (wide,) * 3,
        out_specs=(rows, rows),
        check_vma=False,
    )
```

```python
import functools

import jax
import jax.numpy as jnp
from jax import lax
from jax.experimental import pallas as pl
from jax.experimental.pallas import tpu as pltpu
from jax.sharding import PartitionSpec as P

EPSILON = 1e-06
GROUP = ("dp", "expert")
BLOCKS = 8


def from_behind(value, axis, steps):
    count = lax.axis_size(axis)
    pairs = [(source, (source + steps) % count) for source in range(count)]
    return lax.ppermute(value, axis, pairs)


def normalize(inputs, norm_scale):
    values = inputs.astype(jnp.float32)
    inv_rms = lax.rsqrt(jnp.mean(values * values, axis=-1, keepdims=True) + EPSILON)
    return ((values * inv_rms * norm_scale).astype(jnp.bfloat16), values, inv_rms)


def dense_weights(routes, weights, experts_total):
    onehot = routes[:, :, None] == jnp.arange(experts_total, dtype=jnp.int32)
    return jnp.sum(jnp.where(onehot, weights[:, :, None], 0.0), axis=1)


def dot(a, b):
    return jnp.dot(a, b, preferred_element_type=jnp.float32)


def dot_t(a, b):
    return lax.dot_general(a, b, (((1,), (1,)), ((), ())), preferred_element_type=jnp.float32)


def by_blocks(work, block, *operands):
    count = operands[0].shape[0] // block
    if count == 1:
        return work(*operands)
    cut = [value.reshape(count, block, *value.shape[1:]) for value in operands]
    made = lax.map(lambda parts: work(*parts), tuple(cut))
    return made.reshape(count * block, made.shape[-1])


def body(
    fwd_inputs,
    fwd_routes,
    fwd_weights,
    bwd_inputs,
    bwd_cotangent,
    bwd_routes,
    bwd_weights,
    norm_gain,
    w_gate,
    w_up,
    w_down,
):
    local_experts = w_gate.shape[1]
    experts_total = local_experts * lax.axis_size("dp") * lax.axis_size("expert")
    first = local_experts * (lax.axis_index("dp") * lax.axis_size("expert") + lax.axis_index("expert"))
    norm_scale = norm_gain[0]
    both = jnp.stack(
        [
            dense_weights(fwd_routes[0], fwd_weights[0], experts_total),
            dense_weights(bwd_routes[0], bwd_weights[0], experts_total),
        ],
        axis=1,
    )
    both = lax.all_gather(both, GROUP, axis=0, tiled=True)
    both = lax.dynamic_slice_in_dim(both, first, local_experts, axis=2)
    normed_fwd = normalize(fwd_inputs[0], norm_scale)[0]
    normed_bwd, back_values, back_rms = normalize(bwd_inputs[0], norm_scale)
    fwd_rows = lax.all_gather(normed_fwd, GROUP, axis=0, tiled=True)
    bwd_rows = lax.all_gather(normed_bwd, GROUP, axis=0, tiled=True)
    cot_rows = lax.all_gather(bwd_cotangent[0], GROUP, axis=0, tiled=True)

    def forward(rows, factors):
        partial = 0.0
        for e in range(local_experts):
            gate = dot(rows, w_gate[0, e])
            up = dot(rows, w_up[0, e])
            act = gate * jax.nn.sigmoid(gate) * up * factors[:, e : e + 1]
            partial = partial + dot(act.astype(jnp.bfloat16), w_down[0, e])
        return partial.astype(jnp.bfloat16)

    def backward(rows, cotangents, factors):
        partial = 0.0
        for e in range(local_experts):
            gate = dot(rows, w_gate[0, e])
            up = dot(rows, w_up[0, e])
            hidden = dot_t(cotangents, w_down[0, e]) * factors[:, e : e + 1]
            q = jax.nn.sigmoid(gate)
            d_gate = (hidden * up * q * (1.0 + gate * (1.0 - q))).astype(jnp.bfloat16)
            d_up = (hidden * gate * q).astype(jnp.bfloat16)
            partial = partial + dot_t(d_gate, w_gate[0, e]) + dot_t(d_up, w_up[0, e])
        return partial.astype(jnp.bfloat16)

    block = BLOCKS * fwd_inputs.shape[1]
    partial = by_blocks(forward, block, fwd_rows, both[:, 0])
    combined = lax.psum_scatter(partial, GROUP, scatter_dimension=0, tiled=True)
    section_out = (fwd_inputs[0].astype(jnp.float32) + combined.astype(jnp.float32)).astype(jnp.bfloat16)
    next_forward = from_behind(section_out[None], "segment", 1)

    partial = by_blocks(backward, block, bwd_rows, cot_rows, both[:, 1])
    norm_grad = lax.psum_scatter(
        partial, GROUP, scatter_dimension=0, tiled=True
    ).astype(jnp.float32)
    scaled = norm_scale * norm_grad
    section_grad = (
        bwd_cotangent[0].astype(jnp.float32)
        + back_rms * scaled
        - back_values * back_rms**3 * jnp.mean(back_values * scaled, axis=-1, keepdims=True)
    ).astype(jnp.bfloat16)
    prev_grad = from_behind(section_grad[None], "segment", -1)
    return (next_forward, prev_grad)


LANES = 128
VMEM_BYTES = 52 * 2**20


def remote(src, dst, send, recv, device):
    return pltpu.make_async_remote_copy(
        src_ref=src, dst_ref=dst, send_sem=send, recv_sem=recv,
        device_id=device, device_id_type=pl.DeviceIdType.MESH,
    )


def kernel(
    n_seg, n_dp, experts_total,
    fwd_ref, froute_ref, fweight_ref, bwd_ref, cot_ref, broute_ref, bweight_ref, gain_ref,
    gate_hbm, up_hbm, down_hbm, next_ref, prev_ref,
    gate_w, up_w, down_w, rows, factors, part, mate, summed, landed, hidden, act_a, act_b, outs,
    load_sem, fac_send, fac_recv, row_send, row_recv, mate_send, mate_recv,
    psend, precv, qsend, qrecv, shift_send, shift_recv,
):
    seg, dp, ex = lax.axis_index("segment"), lax.axis_index("dp"), lax.axis_index("expert")
    me = dp * 2 + ex
    group = n_dp * 2
    other = 1 - ex
    tokens, width = cot_ref.shape
    local, _, inner = gate_w.shape
    cut = 2 if tokens % 32 == 0 else 1
    halves = [pl.ds(h * (tokens // cut), tokens // cut) for h in range(cut)]
    ahead, behind = lax.rem(seg + 1, n_seg), lax.rem(seg + n_seg - 1, n_seg)

    loads = [
        pltpu.make_async_copy(src, dst, load_sem.at[i])
        for i, (src, dst) in enumerate(((down_hbm, down_w), (gate_hbm, gate_w), (up_hbm, up_w)))
    ]
    for copy in loads:
        copy.start()

    def member(k):
        p = lax.rem(me + k, group)
        return (seg, p // 2, lax.rem(p, 2))

    barrier = pltpu.get_barrier_semaphore()
    for k in range(1, group):
        pl.semaphore_signal(barrier, inc=1, device_id=member(k), device_id_type=pl.DeviceIdType.MESH)
    for s in (ahead, behind):
        pl.semaphore_signal(barrier, inc=1, device_id=(s, dp, ex), device_id_type=pl.DeviceIdType.MESH)
    pl.semaphore_wait(barrier, group + 1)

    def start_rows(t):
        copies = []
        own = rows.at[t, dp, ex]
        for k in range(1, n_dp):
            copies.append(remote(own, own, row_send.at[t, k], row_recv.at[t, k], (seg, lax.rem(dp + k, n_dp), ex)))
        copies.append(remote(own, own, mate_send.at[t, 0], mate_recv.at[t, 0], (seg, dp, other)))
        for copy in copies:
            copy.start()
        return copies

    def finish_rows(t, copies):
        passed = [copies[-1]]
        for k in range(1, n_dp):
            copies[k - 1].wait_recv()
            slot = rows.at[t, lax.rem(dp + n_dp - k, n_dp), ex]
            copy = remote(slot, slot, mate_send.at[t, k], mate_recv.at[t, k], (seg, dp, other))
            copy.start()
            passed.append(copy)
        for copy in passed:
            copy.wait_recv()
        return copies[:-1] + passed

    rows[0, dp, ex] = cot_ref[...]
    cot_copies = start_rows(0)
    rows[1, dp, ex] = normalize(bwd_ref[...], gain_ref[...])[0]
    bwd_copies = start_rows(1)

    lane = lax.broadcasted_iota(jnp.int32, (tokens, LANES), 1)
    dense = jnp.zeros((tokens, LANES), jnp.float32)
    for base, routes, weights in ((0, froute_ref, fweight_ref), (experts_total, broute_ref, bweight_ref)):
        for k in range(routes.shape[1]):
            hit = lane == routes[:, k : k + 1] + base
            dense = dense + jnp.where(hit, weights[:, k : k + 1], 0.0)
    factors[me] = dense
    fac_copies = [
        remote(factors.at[me], factors.at[me], fac_send.at[k], fac_recv.at[k], member(k)) for k in range(1, group)
    ]
    for copy in fac_copies:
        copy.start()
    rows[2, dp, ex] = normalize(fwd_ref[...], gain_ref[...])[0]
    fwd_copies = start_rows(2)

    pair = 2 * tokens

    def column(d, base, e):
        table = factors[pl.ds(d * 2, 2)].reshape(pair, LANES)
        spot = lax.broadcasted_iota(jnp.int32, (pair, LANES), 1) == base + me * local + e
        return jnp.sum(jnp.where(spot, table, 0.0), axis=1, keepdims=True)

    def scatter(t, product):
        mates, sent = [None] * n_dp, []

        def pass_on(k):
            q = lax.rem(dp + k, n_dp)
            mates[k].wait_recv()
            if k:
                both = part[t, q, ex].astype(jnp.float32) + mate[t, q].astype(jnp.float32)
                summed[t, k] = both.astype(jnp.bfloat16)
                for h, at in enumerate(halves):
                    copy = remote(
                        summed.at[t, k, at], landed.at[t, k, at], qsend.at[t, k, h], qrecv.at[t, k, h], (seg, q, ex)
                    )
                    copy.start()
                    sent.append(copy)

        order = list(range(1, n_dp)) + [0]
        for i, k in enumerate(order):
            q = lax.rem(dp + k, n_dp)
            product(q)
            mates[k] = remote(
                part.at[t, q, other], mate.at[t, q], psend.at[t, k], precv.at[t, k], (seg, dp, other)
            )
            mates[k].start()
            if i:
                pass_on(order[i - 1])
        pass_on(order[-1])
        return mates, sent

    tile = 512 if width % 512 == 0 else LANES

    def tiles(t, q, make):
        def step(i, carry):
            at = pl.ds(pl.multiple_of(i * tile, tile), tile)
            made = make(q, at).astype(jnp.bfloat16)
            part[t, q, :, :, at] = made.reshape(2, tokens, tile)
            return carry

        lax.fori_loop(0, width // tile, step, 0)

    def each(work):
        def step(i, carry):
            work(i // local, lax.rem(i, local))
            return carry

        lax.fori_loop(0, n_dp * local, step, 0)

    def cot_work(d, e):
        hidden[d, e] = dot_t(rows[0, d].reshape(pair, width), down_w[e])

    def bwd_work(d, e):
        x = rows[1, d].reshape(pair, width)
        gate, up = dot(x, gate_w[e]), dot(x, up_w[e])
        back = hidden[d, e] * column(d, experts_total, e)
        q = jax.nn.sigmoid(gate)
        act_a[d, e] = (back * up * q * (1.0 + gate * (1.0 - q))).astype(jnp.bfloat16)
        act_b[d, e] = (back * gate * q).astype(jnp.bfloat16)

    def bwd_product(q):
        def make(q, at):
            total = 0.0
            for e in range(local):
                total = total + dot_t(act_a[q, e], gate_w[e, at, :]) + dot_t(act_b[q, e], up_w[e, at, :])
            return total

        tiles(0, q, make)

    def fwd_work(d, e):
        x = rows[2, d].reshape(pair, width)
        gate, up = dot(x, gate_w[e]), dot(x, up_w[e])
        act_a[d, e] = (gate * jax.nn.sigmoid(gate) * up * column(d, 0, e)).astype(jnp.bfloat16)

    def fwd_product(q):
        def make(q, at):
            total = 0.0
            for e in range(local):
                total = total + dot(act_a[q, e], down_w[e, :, at])
            return total

        tiles(1, q, make)

    def gathered(t, sent, h):
        at = halves[h]
        total = part[t, dp, ex, at].astype(jnp.float32) + mate[t, dp, at].astype(jnp.float32)
        for copy in sent[h::cut]:
            copy.wait_recv()
        for k in range(1, n_dp):
            total = total + landed[t, k, at].astype(jnp.float32)
        return total

    cot_copies = finish_rows(0, cot_copies)
    loads[0].wait()
    each(cot_work)
    bwd_copies = finish_rows(1, bwd_copies)
    for copy in fac_copies:
        copy.wait_recv()
    loads[1].wait()
    loads[2].wait()
    each(bwd_work)
    bwd_mates, bwd_sent = scatter(0, bwd_product)

    fwd_copies = finish_rows(2, fwd_copies)
    each(fwd_work)
    fwd_mates, fwd_sent = scatter(1, fwd_product)

    shifts = []

    def shift(t, h, target, device):
        copy = remote(outs.at[t, halves[h]], target.at[halves[h]], shift_send.at[t, h], shift_recv.at[t, h], device)
        copy.start()
        shifts.append(copy)

    for h, at in enumerate(halves):
        scaled = gain_ref[...] * gathered(0, bwd_sent, h)
        _, values, inv_rms = normalize(bwd_ref[at], gain_ref[...])
        mean = jnp.mean(values * scaled, axis=-1, keepdims=True)
        grad = cot_ref[at].astype(jnp.float32) + inv_rms * scaled - values * inv_rms**3 * mean
        outs[0, at] = grad.astype(jnp.bfloat16)
        shift(0, h, prev_ref, (behind, dp, ex))
    for h, at in enumerate(halves):
        outs[1, at] = (fwd_ref[at].astype(jnp.float32) + gathered(1, fwd_sent, h)).astype(jnp.bfloat16)
        shift(1, h, next_ref, (ahead, dp, ex))
    for copy in cot_copies + bwd_copies + fwd_copies + fac_copies + bwd_mates + fwd_mates + bwd_sent + fwd_sent:
        copy.wait_send()
    for copy in shifts:
        copy.wait()


def fused(n_seg, n_dp, *operands):
    flat = [value[0] for value in operands]
    flat[7] = operands[7]
    tokens, width = flat[0].shape
    local, _, inner = flat[8].shape
    wide, dma = jnp.bfloat16, pltpu.SemaphoreType.DMA
    block = (tokens, width)
    out = jax.ShapeDtypeStruct(block, wide)
    vmem = pl.BlockSpec(memory_space=pltpu.VMEM)
    group = 2 * n_dp
    made = pl.pallas_call(
        functools.partial(kernel, n_seg, n_dp, group * local),
        out_shape=(out, out),
        in_specs=[vmem] * 8 + [pl.BlockSpec(memory_space=pl.ANY)] * 3,
        out_specs=(vmem, vmem),
        scratch_shapes=[
            pltpu.VMEM(flat[8].shape, wide),
            pltpu.VMEM(flat[9].shape, wide),
            pltpu.VMEM(flat[10].shape, wide),
            pltpu.VMEM((3, n_dp, 2) + block, wide),
            pltpu.VMEM((group, tokens, LANES), jnp.float32),
            pltpu.VMEM((2, n_dp, 2) + block, wide),
            pltpu.VMEM((2, n_dp) + block, wide),
            pltpu.VMEM((2, n_dp) + block, wide),
            pltpu.VMEM((2, n_dp) + block, wide),
            pltpu.VMEM((n_dp, local, 2 * tokens, inner), jnp.float32),
            pltpu.VMEM((n_dp, local, 2 * tokens, inner), wide),
            pltpu.VMEM((n_dp, local, 2 * tokens, inner), wide),
            pltpu.VMEM((2,) + block, wide),
            dma((3,)), dma((group,)), dma((group,)),
            dma((3, n_dp)), dma((3, n_dp)), dma((3, n_dp)), dma((3, n_dp)),
            dma((2, n_dp)), dma((2, n_dp)), dma((2, n_dp, 2)), dma((2, n_dp, 2)),
            dma((2, 2)), dma((2, 2)),
        ],
        compiler_params=pltpu.CompilerParams(
            collective_id=0, has_side_effects=True, vmem_limit_bytes=VMEM_BYTES
        ),
    )(*flat)
    return (made[0][None], made[1][None])


def whole(n_seg, n_dp, n_expert, *operands):
    tokens, width = operands[0].shape[1:]
    local = operands[8].shape[1]
    group = n_dp * n_expert
    rows_bytes = group * tokens * width * 2
    small = 9 * rows_bytes + 3 * operands[8].size * 2 <= VMEM_BYTES * 3 // 4
    if n_expert == 2 and n_dp > 1 and n_seg > 1 and 2 * group * local <= LANES and small:
        return fused(n_seg, n_dp, *operands)
    return body(*operands)


def solution(mesh):
    rows = P("segment", GROUP, None)
    wide = P("segment", GROUP, None, None)
    return jax.shard_map(
        functools.partial(whole, mesh.shape["segment"], mesh.shape["dp"], mesh.shape["expert"]),
        mesh=mesh,
        in_specs=(rows,) * 7 + (P("segment", None),) + (wide,) * 3,
        out_specs=(rows, rows),
        check_vma=False,
    )
```
